512 devices in a mesh: row: 16 (over z, core), col: 32 (over y, x).
Axes of the slice: x: 4, y: 8, z: 8, core: 2. Of those that a mesh axis runs over, the one named last changes fastest.
Arguments:
- src_points: float32 [50, 32768], P(None, ('row', 'col')), may hold values from -25 to 25
- dst_points: float32 [50, 98304], P(None, ('col', 'row')), may hold values from -25 to 25
- log_a: float32 [32768], P('row'), may hold values from -1 to 1
- log_b: float32 [98304], P('col'), may hold values from -1 to 1
- dst_potential: float32 [98304], P('col'), may hold values from -6 to 60
Outputs:
- src_potential: float32 [32768], P('row')
- new_potential: float32 [98304], P('col')
The draws below stay inside these ranges and needn't reach their ends.
All inputs are finite; a program needn't handle non-finite values.
Results may differ from the reference program's by a relative error of at most 0.00013.
Values sent between devices are 32-bit elements; how exact they have to be, the bound alone decides.
No kernel may reach another device: no remote copies, remote signals or barrier semaphores. Data moves between devices by JAX's collectives and lax.ppermute only.
A program may use at most 64 MiB of HBM per device.

```python
import math
import jax
import jax.numpy as jnp
from jax import lax

E = 50
NS = 32768
NT = 98304


def point_scales(base):
    return base * (jnp.arange(E, dtype=jnp.float32) + 1.0) ** (-0.25)


def target_cloud(key, base):
    return point_scales(base)[:, None] * jnp.clip(jax.random.normal(key, (E, NT), jnp.float32), -6.0, 6.0)


def draw_dst_points(key, part):
    cloud = target_cloud(key, 0.3)
    return cloud


def draw_src_points(key, part):
    key = jax.random.fold_in(key, 1)
    points = point_scales(0.3)[:, None] * jnp.clip(jax.random.normal(key, (E, NS), jnp.float32), -6.0, 6.0)
    return points


def draw_dst_potential(key, part):
    key = jax.random.fold_in(key, 2)
    return jnp.clip(jax.random.normal(key, (NT,), jnp.float32), -5.0, 5.0)


def level_of(stream_key, extent, split, low, high):
    level = 1.0
    for dim, parts in split:
        steps = jax.random.uniform(jax.random.fold_in(jax.random.fold_in(stream_key, 6), dim), (parts,), jnp.float32, low / len(split), high / len(split))
        level = level * jnp.repeat(jnp.exp(steps), extent[dim] // parts).reshape((-1,) + (1,) * (len(extent) - 1 - dim))
    return level


def setup_inputs(seed: int = 0) -> dict:
    key_list = jax.random.split(jax.random.key(seed), 6)
    return {
        "src_points": draw_src_points(jax.random.fold_in(key_list[5], 71), 0),
        "dst_points": draw_dst_points(jax.random.fold_in(key_list[5], 71), 0),
        "log_a": jnp.clip(jax.random.uniform(key_list[2], (NS,), jnp.float32, -1.0, 1.0) * level_of(key_list[2], (NS,), ((0, 16),), -0.4, 0.0), -1.0, 1.0),
        "log_b": jnp.clip(jax.random.uniform(key_list[3], (NT,), jnp.float32, -1.0, 1.0) * level_of(key_list[3], (NT,), ((0, 32),), -0.4, 0.0), -1.0, 1.0),
        "dst_potential": draw_dst_potential(jax.random.fold_in(key_list[5], 71), 0),
    }


epsilon = 0.5


def cost_rows(points_block, norms_block, targets, target_norms):
    inner = lax.dot_general(points_block, targets, (((0,), (0,)), ((), ())), precision=lax.Precision.HIGHEST, preferred_element_type=jnp.float32)
    return norms_block[:, None] + target_norms[None, :] - 2.0 * inner


def reference(src_points, dst_points, log_a, log_b, dst_potential):
    src_norms = jnp.sum(src_points * src_points, 0)
    dst_norms = jnp.sum(dst_points * dst_points, 0)
    block_rows = math.gcd(NS, 512)
    blocks = NS // block_rows
    src_blocks = src_points.reshape(E, blocks, block_rows).transpose(1, 0, 2)
    norm_blocks = src_norms.reshape(blocks, block_rows)
    weight_blocks = log_a.reshape(blocks, block_rows)

    def advance(running, operands):
        points_block, norms_block, weight_block = operands
        costs = cost_rows(points_block, norms_block, dst_points, dst_norms)
        scores = (dst_potential[None, :] - costs) / epsilon
        highest = jnp.max(scores, 1)
        summed = jnp.sum(jnp.exp(scores - highest[:, None]), 1)
        potential_block = epsilon * weight_block - epsilon * (highest + jnp.log(summed))
        col_scores = (potential_block[:, None] - costs) / epsilon
        col_high = jnp.max(col_scores, 0)
        col_sum = jnp.sum(jnp.exp(col_scores - col_high[None, :]), 0)
        merged_high = jnp.maximum(running[0], col_high)
        merged_sum = running[1] * jnp.exp(running[0] - merged_high) + col_sum * jnp.exp(col_high - merged_high)
        return (merged_high, merged_sum), potential_block

    initial = (jnp.full((NT,), -jnp.inf, jnp.float32), jnp.zeros((NT,), jnp.float32))
    (final_high, final_sum), potentials = lax.scan(advance, initial, (src_blocks, norm_blocks, weight_blocks))
    src_potential = potentials.reshape(NS)
    new_potential = epsilon * log_b - epsilon * (final_high + jnp.log(final_sum))
    return src_potential, new_potential
```

```python
import math

import jax
import jax.numpy as jnp
from jax import lax
from jax.experimental import pallas as pl
from jax.experimental.pallas import tpu as pltpu
from jax.sharding import PartitionSpec as P

epsilon = 0.5
per_eps = math.log2(math.e) / epsilon
point_scale = math.sqrt(2.0 * per_eps)
eps_ln2 = epsilon * math.log(2.0)
log2e = math.log2(math.e)
too_large = 2.0**100
too_small = 2.0**-100
vmem_limit = 40 * 1024 * 1024

lanes = 128
half = 64
depth = 256


def lane_index(shape):
    return lax.broadcasted_iota(jnp.int32, shape, 1)


def row_index(shape):
    return lax.broadcasted_iota(jnp.int32, shape, 0)


def rounded(value):
    return value.astype(jnp.bfloat16).astype(jnp.float32)


def pieces(value):
    first = rounded(value)
    second = rounded(value - first)
    third = rounded(value - first - second)
    return first, second, third


def folded(points):
    left = jnp.concatenate([points[0:24], jnp.zeros((2, half), jnp.float32)], 0)
    return jnp.concatenate([left, points[24:50]], 1)


def unfolded(first, second):
    left = lane_index(first.shape) < half
    low = jnp.where(left, first, pltpu.roll(second, half, 1))
    high = jnp.where(left, pltpu.roll(first, half, 1), second)
    return low, high


def pack_kernel(src_ref, dst_ref, src_out, dst_out):
    odd = lax.rem(lax.axis_index("row"), 2) == 1
    src = folded(src_ref[...])
    src = jnp.concatenate([src, jnp.zeros((6, lanes), jnp.float32)], 0)
    src_out[...] = jnp.broadcast_to(src[None], src_out.shape)
    points = dst_ref[...]
    whole = jnp.where(odd, points[:, half : half + lanes], points[:, :lanes])
    rest = jnp.where(odd, points[:, :half], points[:, lanes:])
    dst_out[...] = jnp.concatenate([whole, folded(rest), jnp.zeros((4, lanes), jnp.float32)], 0)


def split(points):
    scaled = points * point_scale
    high = rounded(scaled)
    low = rounded(scaled - high)
    exact = high + low
    return high, low, jnp.sum(exact * exact, 0, keepdims=True)


def with_rows(block, first, values):
    rows = row_index(block.shape)
    for offset, value in enumerate(values):
        block = jnp.where(rows == first + offset, value, block)
    return block


def build_sources(src_ref, b_ref, norm_ref):
    pad = jnp.zeros((8, lanes), jnp.float32)
    norms = []
    for k in range(src_ref.shape[0] // 2):
        low, high = unfolded(src_ref[2 * k], src_ref[2 * k + 1])
        first, second, norm = split(jnp.concatenate([low[0:24], high], 0))
        norms.append(norm)
        extra = with_rows(first, 50, [1.0, 1.0, 1.0])
        columns = slice(lanes * k, lanes * (k + 1))
        second = jnp.concatenate([second, pad], 0).astype(jnp.bfloat16)
        b_ref[0:64, columns] = jnp.concatenate([extra, pad], 0).astype(jnp.bfloat16)
        b_ref[64:128, columns] = jnp.concatenate([first, pad], 0).astype(jnp.bfloat16)
        b_ref[128:192, columns] = second
        b_ref[192:256, columns] = second
    norm_ref[...] = jnp.concatenate(norms, 0)


def build_targets(dst_ref, potential_ref, a_ref):
    pad = jnp.zeros((8, lanes), jnp.float32)
    gap = jnp.zeros((6, lanes), jnp.float32)
    for pair in range(dst_ref.shape[0] // 2):
        even = dst_ref[2 * pair]
        odd = dst_ref[2 * pair + 1]
        low, high = unfolded(even[50:76], odd[50:76])
        middle = jnp.concatenate([low[0:24], high], 0)
        for part, points in enumerate([even[0:50], middle, odd[0:50]]):
            tile = 3 * pair + part
            first, second, norm = split(jnp.concatenate([points, gap], 0))
            bias = potential_ref[tile : tile + 1, :] * per_eps - 0.5 * norm
            extra = with_rows(first, 50, list(pieces(bias)) + [1.0, 1.0, 1.0])
            turned = jnp.concatenate([extra, pad, second, pad], 0).T
            column = lane_index(turned.shape)
            plain = jnp.where((column >= 50) & (column < 56), 0.0, turned)
            rows = slice(lanes * tile, lanes * (tile + 1))
            a_ref[rows, 0:lanes] = turned.astype(jnp.bfloat16)
            a_ref[rows, lanes : 2 * lanes] = plain.astype(jnp.bfloat16)


def dot(left, right):
    return jnp.dot(left, right, preferred_element_type=jnp.float32)


def biased_rows(rows16, bias):
    block = with_rows(rows16.astype(jnp.float32), 5, pieces(bias))
    return block.astype(jnp.bfloat16)


def as_tiles(row):
    return jnp.concatenate(
        [row[:, lanes * k : lanes * (k + 1)] for k in range(row.shape[1] // lanes)], 0
    )


def as_row(tiles):
    return jnp.concatenate([tiles[k : k + 1, :] for k in range(tiles.shape[0])], 1)


def source_kernel(src_ref, dst_ref, potential_ref, lse_ref, a_ref, b_ref, norm_ref, sum_ref):
    build_sources(src_ref, b_ref, norm_ref)
    build_targets(dst_ref, potential_ref, a_ref)
    targets = a_ref.shape[0]
    sources = b_ref.shape[1]
    width = 256
    chunk = 512
    shift = jnp.concatenate(
        [
            jnp.max(dot(a_ref[0:lanes, :], b_ref[:, width * n : width * (n + 1)]), 0, keepdims=True)
            for n in range(sources // width)
        ],
        1,
    )
    b_ref[48:64, :] = biased_rows(b_ref[48:64, :], -shift)
    for n in range(sources // width):
        columns = slice(width * n, width * (n + 1))
        block = b_ref[:, columns]

        def add(step, total):
            rows = pl.ds(pl.multiple_of(step * chunk, chunk), chunk)
            terms = jnp.exp2(dot(a_ref[rows, :], block))
            return total + jnp.sum(terms.reshape(chunk // 8, 8, width), 0)

        total = lax.fori_loop(0, targets // chunk, add, jnp.zeros((8, width), jnp.float32))
        sum_ref[0:1, columns] = jnp.sum(total, 0, keepdims=True)
    total = sum_ref[0:1, :]
    sum_ref[1:2, :] = shift + jnp.log2(total)

    @pl.when(jnp.logical_not(jnp.max(jnp.where(total <= too_large, 0.0, 1.0)) < 0.5))
    def exact():
        for n in range(sources // width):
            columns = slice(width * n, width * (n + 1))
            block = b_ref[:, columns]

            def rows_of(step):
                return pl.ds(pl.multiple_of(step * lanes, lanes), lanes)

            def highest(step, high):
                scores = dot(a_ref[rows_of(step), :], block)
                return jnp.maximum(high, jnp.max(scores, 0, keepdims=True))

            high = lax.fori_loop(
                0, targets // lanes, highest, jnp.full((1, width), -jnp.inf, jnp.float32)
            )

            def add(step, total):
                scores = dot(a_ref[rows_of(step), :], block)
                return total + jnp.sum(jnp.exp2(scores - high), 0, keepdims=True)

            total = lax.fori_loop(0, targets // lanes, add, jnp.zeros((1, width), jnp.float32))
            sum_ref[1:2, columns] = shift[:, columns] + (high + jnp.log2(total))

    lse_ref[...] = jnp.broadcast_to(as_tiles(sum_ref[1:2, :])[None], lse_ref.shape)


def target_kernel(lse_ref, log_a_ref, norm_ref, a_ref, b_ref, src_out, lse_out, acc_ref):
    targets = a_ref.shape[0]
    sources = b_ref.shape[1]
    width = 256
    chunk = 512
    parts = lse_ref[...]
    high = jnp.max(parts, 0)
    lse = high + jnp.log2(jnp.sum(jnp.exp2(parts - high[None]), 0))
    src_out[...] = epsilon * log_a_ref[...] - eps_ln2 * (lse - 0.5 * norm_ref[...])
    middle = biased_rows(b_ref[48:64, :], as_row(log2e * log_a_ref[...] - lse))

    def block_of(n):
        columns = slice(width * n, width * (n + 1))
        return jnp.concatenate(
            [b_ref[0:48, columns], middle[:, columns], b_ref[64:depth, columns]], 0
        )

    for n in range(sources // width):
        block = block_of(n)

        def add(step, carry):
            rows = pl.ds(pl.multiple_of(step * chunk, chunk), chunk)
            terms = jnp.exp2(dot(a_ref[rows, :], block))
            terms = terms[:, 0:lanes] + terms[:, lanes:]
            acc_ref[rows, :] = terms if n == 0 else acc_ref[rows, :] + terms
            return carry

        lax.fori_loop(0, targets // chunk, add, 0)
    totals = jnp.concatenate(
        [
            jnp.sum(acc_ref[lanes * t : lanes * (t + 1), :].T, 0, keepdims=True)
            for t in range(targets // lanes)
        ],
        0,
    )
    lse_out[...] = jnp.log2(totals)

    @pl.when(jnp.logical_not(jnp.max(jnp.where(totals >= too_small, 0.0, 1.0)) < 0.5))
    def exact():
        def one(tile, carry):
            left = a_ref[pl.ds(pl.multiple_of(tile * lanes, lanes), lanes), :]
            high = jnp.full((lanes, 1), -jnp.inf, jnp.float32)
            for n in range(sources // width):
                scores = dot(left, block_of(n))
                high = jnp.maximum(high, jnp.max(scores, 1, keepdims=True))
            total = jnp.zeros((lanes, 1), jnp.float32)
            for n in range(sources // width):
                scores = dot(left, block_of(n))
                total = total + jnp.sum(jnp.exp2(scores - high), 1, keepdims=True)
            result = jnp.broadcast_to(high + jnp.log2(total), (lanes, lanes)).T
            lse_out[pl.ds(tile, 1), :] = result[0:1, :]
            return carry

        lax.fori_loop(0, targets // lanes, one, 0)


def join_kernel(lse_ref, log_b_ref, potential_ref, out_ref):
    parts = lse_ref[...]
    high = jnp.max(parts, 0)
    lse = high + jnp.log2(jnp.sum(jnp.exp2(parts - high[None]), 0))
    out_ref[...] = epsilon * log_b_ref[...] + potential_ref[...] - eps_ln2 * lse


def shape(*dims, dtype=jnp.float32):
    return jax.ShapeDtypeStruct(dims, dtype)


def call(kernel, outs, scratch=(), cost=None):
    vmem = pl.BlockSpec(memory_space=pltpu.VMEM)
    many = isinstance(outs, tuple)
    return pl.pallas_call(
        kernel,
        out_shape=outs,
        out_specs=tuple(vmem for _ in outs) if many else vmem,
        scratch_shapes=scratch,
        compiler_params=pltpu.CompilerParams(vmem_limit_bytes=vmem_limit),
        cost_estimate=cost,
    )


def local(src_points, dst_points, log_a, log_b, dst_potential):
    rows = lax.axis_size("row")
    cols = lax.axis_size("col")
    sources = log_a.shape[0]
    targets = log_b.shape[0]
    log_a = log_a.reshape(sources // lanes, lanes)
    log_b = log_b.reshape(targets // lanes, lanes)
    potential = dst_potential.reshape(targets // lanes, lanes)
    pairs = sources * targets
    cost = pl.CostEstimate(
        flops=2 * depth * pairs, transcendentals=pairs, bytes_accessed=4 * depth * (sources + targets)
    )

    src, dst = call(pack_kernel, (shape(cols, 32, lanes), shape(80, lanes)))(src_points, dst_points)
    src = lax.all_to_all(src, "col", 0, 0, tiled=True)
    dst = lax.all_gather(dst, "row")

    lse, a, b, norms = call(
        source_kernel,
        (
            shape(cols, sources // lanes, lanes),
            shape(targets, depth, dtype=jnp.bfloat16),
            shape(depth, sources, dtype=jnp.bfloat16),
            shape(sources // lanes, lanes),
        ),
        [pltpu.VMEM((8, sources), jnp.float32)],
        cost,
    )(src, dst, potential)

    lse = lax.all_to_all(lse, "col", 0, 0, tiled=True)
    src_potential, lse = call(
        target_kernel,
        (shape(sources // lanes, lanes), shape(targets // lanes, lanes)),
        [pltpu.VMEM((targets, lanes), jnp.float32)],
        cost,
    )(lse, log_a, norms, a, b)

    lse = lax.all_gather(lse, "row")
    new_potential = call(join_kernel, shape(targets // lanes, lanes))(lse, log_b, potential)
    return src_potential.reshape(sources), new_potential.reshape(targets)


def solution(mesh):
    return jax.shard_map(
        local,
        mesh=mesh,
        in_specs=(P(None, ("row", "col")), P(None, ("col", "row")), P("row"), P("col"), P("col")),
        out_specs=(P("row"), P("col")),
        check_vma=False,
    )
```

```python
import math

import jax
import jax.numpy as jnp
from jax import lax
from jax.experimental import pallas as pl
from jax.experimental.pallas import tpu as pltpu
from jax.sharding import PartitionSpec as P

epsilon = 0.5
per_eps = math.log2(math.e) / epsilon
point_scale = math.sqrt(2.0 * per_eps)
eps_ln2 = epsilon * math.log(2.0)
log2e = math.log2(math.e)
too_large = 2.0**100
too_small = 2.0**-100
vmem_limit = 40 * 1024 * 1024

lanes = 128
half = 64
depth = 256


def lane_index(shape):
    return lax.broadcasted_iota(jnp.int32, shape, 1)


def row_index(shape):
    return lax.broadcasted_iota(jnp.int32, shape, 0)


def rounded(value):
    return value.astype(jnp.bfloat16).astype(jnp.float32)


def pieces(value):
    first = rounded(value)
    second = rounded(value - first)
    third = rounded(value - first - second)
    return first, second, third


def folded(points):
    left = jnp.concatenate([points[0:24], jnp.zeros((2, half), jnp.float32)], 0)
    return jnp.concatenate([left, points[24:50]], 1)


def unfolded(first, second):
    left = lane_index(first.shape) < half
    low = jnp.where(left, first, pltpu.roll(second, half, 1))
    high = jnp.where(left, pltpu.roll(first, half, 1), second)
    return low, high


def pack_kernel(src_ref, dst_ref, src_out, dst_out):
    odd = lax.rem(lax.axis_index("row"), 2) == 1
    src = folded(src_ref[...])
    src = jnp.concatenate([src, jnp.zeros((6, lanes), jnp.float32)], 0)
    src_out[...] = jnp.broadcast_to(src[None], src_out.shape)
    points = dst_ref[...]
    whole = jnp.where(odd, points[:, half : half + lanes], points[:, :lanes])
    rest = jnp.where(odd, points[:, :half], points[:, lanes:])
    dst_out[...] = jnp.concatenate([whole, folded(rest), jnp.zeros((4, lanes), jnp.float32)], 0)


def split(points):
    scaled = points * point_scale
    high = rounded(scaled)
    low = rounded(scaled - high)
    exact = high + low
    return high, low, jnp.sum(exact * exact, 0, keepdims=True)


def with_rows(block, first, values):
    rows = row_index(block.shape)
    for offset, value in enumerate(values):
        block = jnp.where(rows == first + offset, value, block)
    return block


def build_sources(src_ref, b_ref, norm_ref):
    pad = jnp.zeros((8, lanes), jnp.float32)
    norms = []
    for k in range(src_ref.shape[0] // 2):
        low, high = unfolded(src_ref[2 * k], src_ref[2 * k + 1])
        first, second, norm = split(jnp.concatenate([low[0:24], high], 0))
        norms.append(norm)
        extra = with_rows(first, 50, [1.0, 1.0, 1.0])
        columns = slice(lanes * k, lanes * (k + 1))
        second = jnp.concatenate([second, pad], 0).astype(jnp.bfloat16)
        b_ref[0:64, columns] = jnp.concatenate([extra, pad], 0).astype(jnp.bfloat16)
        b_ref[64:128, columns] = jnp.concatenate([first, pad], 0).astype(jnp.bfloat16)
        b_ref[128:192, columns] = second
        b_ref[192:256, columns] = second
    norm_ref[...] = jnp.concatenate(norms, 0)


def build_targets(dst_ref, potential_ref, a_ref):
    pad = jnp.zeros((8, lanes), jnp.float32)
    gap = jnp.zeros((6, lanes), jnp.float32)
    for pair in range(dst_ref.shape[0] // 2):
        even = dst_ref[2 * pair]
        odd = dst_ref[2 * pair + 1]
        low, high = unfolded(even[50:76], odd[50:76])
        middle = jnp.concatenate([low[0:24], high], 0)
        for part, points in enumerate([even[0:50], middle, odd[0:50]]):
            tile = 3 * pair + part
            first, second, norm = split(jnp.concatenate([points, gap], 0))
            bias = potential_ref[tile : tile + 1, :] * per_eps - 0.5 * norm
            extra = with_rows(first, 50, list(pieces(bias)) + [1.0, 1.0, 1.0])
            turned = jnp.concatenate([extra, pad, second, pad], 0).T
            column = lane_index(turned.shape)
            plain = jnp.where((column >= 50) & (column < 56), 0.0, turned)
            rows = slice(lanes * tile, lanes * (tile + 1))
            a_ref[rows, 0:lanes] = turned.astype(jnp.bfloat16)
            a_ref[rows, lanes : 2 * lanes] = plain.astype(jnp.bfloat16)


def dot(left, right):
    return jnp.dot(left, right, preferred_element_type=jnp.float32)


def biased_rows(rows16, bias):
    block = with_rows(rows16.astype(jnp.float32), 5, pieces(bias))
    return block.astype(jnp.bfloat16)


def as_tiles(row):
    return jnp.concatenate(
        [row[:, lanes * k : lanes * (k + 1)] for k in range(row.shape[1] // lanes)], 0
    )


def as_row(tiles):
    return jnp.concatenate([tiles[k : k + 1, :] for k in range(tiles.shape[0])], 1)


def source_kernel(src_ref, dst_ref, potential_ref, lse_ref, a_ref, b_ref, norm_ref, sum_ref):
    build_sources(src_ref, b_ref, norm_ref)
    build_targets(dst_ref, potential_ref, a_ref)
    targets = a_ref.shape[0]
    sources = b_ref.shape[1]
    width = 256
    shift = jnp.concatenate(
        [
            jnp.max(dot(a_ref[0:lanes, :], b_ref[:, width * n : width * (n + 1)]), 0, keepdims=True)
            for n in range(sources // width)
        ],
        1,
    )
    b_ref[48:64, :] = biased_rows(b_ref[48:64, :], -shift)
    for n in range(sources // width):
        columns = slice(width * n, width * (n + 1))
        terms = jnp.exp2(dot(a_ref[...], b_ref[:, columns]))
        total = jnp.sum(terms.reshape(targets // 8, 8, width), 0)
        sum_ref[0:1, columns] = jnp.sum(total, 0, keepdims=True)
    total = sum_ref[0:1, :]
    sum_ref[1:2, :] = shift + jnp.log2(total)

    @pl.when(jnp.logical_not(jnp.max(jnp.where(total <= too_large, 0.0, 1.0)) < 0.5))
    def exact():
        for n in range(sources // width):
            columns = slice(width * n, width * (n + 1))
            block = b_ref[:, columns]

            def rows_of(step):
                return pl.ds(pl.multiple_of(step * lanes, lanes), lanes)

            def highest(step, high):
                scores = dot(a_ref[rows_of(step), :], block)
                return jnp.maximum(high, jnp.max(scores, 0, keepdims=True))

            high = lax.fori_loop(
                0, targets // lanes, highest, jnp.full((1, width), -jnp.inf, jnp.float32)
            )

            def add(step, total):
                scores = dot(a_ref[rows_of(step), :], block)
                return total + jnp.sum(jnp.exp2(scores - high), 0, keepdims=True)

            total = lax.fori_loop(0, targets // lanes, add, jnp.zeros((1, width), jnp.float32))
            sum_ref[1:2, columns] = shift[:, columns] + (high + jnp.log2(total))

    lse_ref[...] = jnp.broadcast_to(as_tiles(sum_ref[1:2, :])[None], lse_ref.shape)


def target_kernel(lse_ref, log_a_ref, norm_ref, a_ref, b_ref, src_out, lse_out, acc_ref):
    targets = a_ref.shape[0]
    sources = b_ref.shape[1]
    width = 256
    parts = lse_ref[...]
    high = jnp.max(parts, 0)
    lse = high + jnp.log2(jnp.sum(jnp.exp2(parts - high[None]), 0))
    src_out[...] = epsilon * log_a_ref[...] - eps_ln2 * (lse - 0.5 * norm_ref[...])
    middle = biased_rows(b_ref[48:64, :], as_row(log2e * log_a_ref[...] - lse))

    def block_of(n):
        columns = slice(width * n, width * (n + 1))
        return jnp.concatenate(
            [b_ref[0:48, columns], middle[:, columns], b_ref[64:depth, columns]], 0
        )

    for n in range(sources // width):
        terms = jnp.exp2(dot(a_ref[...], block_of(n)))
        terms = terms[:, 0:lanes] + terms[:, lanes:]
        acc_ref[...] = terms if n == 0 else acc_ref[...] + terms
    totals = jnp.concatenate(
        [
            jnp.sum(acc_ref[lanes * t : lanes * (t + 1), :].T, 0, keepdims=True)
            for t in range(targets // lanes)
        ],
        0,
    )
    lse_out[...] = jnp.log2(totals)

    @pl.when(jnp.logical_not(jnp.max(jnp.where(totals >= too_small, 0.0, 1.0)) < 0.5))
    def exact():
        def one(tile, carry):
            left = a_ref[pl.ds(pl.multiple_of(tile * lanes, lanes), lanes), :]
            high = jnp.full((lanes, 1), -jnp.inf, jnp.float32)
            for n in range(sources // width):
                scores = dot(left, block_of(n))
                high = jnp.maximum(high, jnp.max(scores, 1, keepdims=True))
            total = jnp.zeros((lanes, 1), jnp.float32)
            for n in range(sources // width):
                scores = dot(left, block_of(n))
                total = total + jnp.sum(jnp.exp2(scores - high), 1, keepdims=True)
            result = jnp.broadcast_to(high + jnp.log2(total), (lanes, lanes)).T
            lse_out[pl.ds(tile, 1), :] = result[0:1, :]
            return carry

        lax.fori_loop(0, targets // lanes, one, 0)


def join_kernel(lse_ref, log_b_ref, potential_ref, out_ref):
    parts = lse_ref[...]
    high = jnp.max(parts, 0)
    lse = high + jnp.log2(jnp.sum(jnp.exp2(parts - high[None]), 0))
    out_ref[...] = epsilon * log_b_ref[...] + potential_ref[...] - eps_ln2 * lse


def shape(*dims, dtype=jnp.float32):
    return jax.ShapeDtypeStruct(dims, dtype)


def call(kernel, outs, scratch=(), cost=None):
    vmem = pl.BlockSpec(memory_space=pltpu.VMEM)
    many = isinstance(outs, tuple)
    return pl.pallas_call(
        kernel,
        out_shape=outs,
        out_specs=tuple(vmem for _ in outs) if many else vmem,
        scratch_shapes=scratch,
        compiler_params=pltpu.CompilerParams(vmem_limit_bytes=vmem_limit),
        cost_estimate=cost,
    )


def local(src_points, dst_points, log_a, log_b, dst_potential):
    rows = lax.axis_size("row")
    cols = lax.axis_size("col")
    sources = log_a.shape[0]
    targets = log_b.shape[0]
    log_a = log_a.reshape(sources // lanes, lanes)
    log_b = log_b.reshape(targets // lanes, lanes)
    potential = dst_potential.reshape(targets // lanes, lanes)
    pairs = sources * targets
    cost = pl.CostEstimate(
        flops=2 * depth * pairs, transcendentals=pairs, bytes_accessed=4 * depth * (sources + targets)
    )

    src, dst = call(pack_kernel, (shape(cols, 32, lanes), shape(80, lanes)))(src_points, dst_points)
    src = lax.all_to_all(src, "col", 0, 0, tiled=True)
    dst = lax.all_gather(dst, "row")

    lse, a, b, norms = call(
        source_kernel,
        (
            shape(cols, sources // lanes, lanes),
            shape(targets, depth, dtype=jnp.bfloat16),
            shape(depth, sources, dtype=jnp.bfloat16),
            shape(sources // lanes, lanes),
        ),
        [pltpu.VMEM((8, sources), jnp.float32)],
        cost,
    )(src, dst, potential)

    lse = lax.all_to_all(lse, "col", 0, 0, tiled=True)
    src_potential, lse = call(
        target_kernel,
        (shape(sources // lanes, lanes), shape(targets // lanes, lanes)),
        [pltpu.VMEM((targets, lanes), jnp.float32)],
        cost,
    )(lse, log_a, norms, a, b)

    lse = lax.all_gather(lse, "row")
    new_potential = call(join_kernel, shape(targets // lanes, lanes))(lse, log_b, potential)
    return src_potential.reshape(sources), new_potential.reshape(targets)


def solution(mesh):
    return jax.shard_map(
        local,
        mesh=mesh,
        in_specs=(P(None, ("row", "col")), P(None, ("col", "row")), P("row"), P("col"), P("col")),
        out_specs=(P("row"), P("col")),
        check_vma=False,
    )
```

```python
import math

import jax
import jax.numpy as jnp
from jax import lax
from jax.experimental import pallas as pl
from jax.experimental.pallas import tpu as pltpu
from jax.sharding import PartitionSpec as P

epsilon = 0.5
per_eps = math.log2(math.e) / epsilon
point_scale = math.sqrt(2.0 * per_eps)
eps_ln2 = epsilon * math.log(2.0)
log2e = math.log2(math.e)
too_large = 2.0**100
too_small = 2.0**-100
vmem_limit = 32 * 1024 * 1024
vmem_whole = 60 * 1024 * 1024

lanes = 128
half = 64
depth = 256


def lane_index(shape):
    return lax.broadcasted_iota(jnp.int32, shape, 1)


def row_index(shape):
    return lax.broadcasted_iota(jnp.int32, shape, 0)


def rounded(value):
    return value.astype(jnp.bfloat16).astype(jnp.float32)


def pieces(value):
    first = rounded(value)
    second = rounded(value - first)
    third = rounded(value - first - second)
    return first, second, third


def folded(points):
    left = jnp.concatenate([points[0:24], jnp.zeros((2, half), jnp.float32)], 0)
    return jnp.concatenate([left, points[24:50]], 1)


def unfolded(first, second):
    left = lane_index(first.shape) < half
    low = jnp.where(left, first, pltpu.roll(second, half, 1))
    high = jnp.where(left, pltpu.roll(first, half, 1), second)
    return low, high


def pack_kernel(src_hbm, dst_hbm, src_out, dst_out, src_ref, dst_ref, src_sem, dst_sem):
    src_copy = pltpu.make_async_copy(src_hbm, src_ref, src_sem)
    dst_copy = pltpu.make_async_copy(dst_hbm, dst_ref, dst_sem)
    src_copy.start()
    dst_copy.start()
    src_copy.wait()
    src = jnp.concatenate([folded(src_ref[...]), jnp.zeros((6, lanes), jnp.float32)], 0)
    src_out[...] = jnp.broadcast_to(src[None], src_out.shape)
    dst_copy.wait()
    dst_out[0:50, :] = dst_ref[:, :lanes]
    dst_out[50:76, :] = folded(dst_ref[:, lanes:])
    dst_out[76:80, :] = jnp.zeros((4, lanes), jnp.float32)


def swapped(rows):
    return pltpu.roll(rows, half, 1)


def inner_order(tiles):
    left = lane_index((1, lanes)) < half
    rows = []
    for t in range(0, tiles.shape[0], 3):
        second, third = tiles[t + 1 : t + 2], tiles[t + 2 : t + 3]
        rows.append(tiles[t : t + 1])
        rows.append(jnp.where(left, second, third))
        rows.append(swapped(jnp.where(left, third, second)))
    return jnp.concatenate(rows, 0)


def outer_order(tiles):
    left = lane_index((1, lanes)) < half
    turned = swapped(tiles)
    rows = []
    for t in range(0, tiles.shape[0], 3):
        second, third = tiles[t + 1 : t + 2], turned[t + 2 : t + 3]
        rows.append(tiles[t : t + 1])
        rows.append(jnp.where(left, second, third))
        rows.append(jnp.where(left, third, second))
    return jnp.concatenate(rows, 0)


def split(points):
    scaled = points * point_scale
    high = rounded(scaled)
    low = rounded(scaled - high)
    exact = high + low
    return high, low, jnp.sum(exact * exact, 0, keepdims=True)


def with_rows(block, first, values):
    rows = row_index(block.shape)
    for offset, value in enumerate(values):
        block = jnp.where(rows == first + offset, value, block)
    return block


def build_sources(src_ref, b_ref, norm_ref):
    pad = jnp.zeros((8, lanes), jnp.float32)
    norms = []
    for k in range(src_ref.shape[0] // 2):
        low, high = unfolded(src_ref[2 * k], src_ref[2 * k + 1])
        first, second, norm = split(jnp.concatenate([low[0:24], high], 0))
        norms.append(norm)
        extra = with_rows(first, 50, [1.0, 1.0, 1.0])
        columns = slice(lanes * k, lanes * (k + 1))
        second = jnp.concatenate([second, pad], 0).astype(jnp.bfloat16)
        b_ref[0:64, columns] = jnp.concatenate([extra, pad], 0).astype(jnp.bfloat16)
        b_ref[64:128, columns] = jnp.concatenate([first, pad], 0).astype(jnp.bfloat16)
        b_ref[128:192, columns] = second
        b_ref[192:256, columns] = second
    norm_ref[...] = jnp.concatenate(norms, 0)


def build_targets(dst_ref, potential_ref, a_ref):
    pad = jnp.zeros((8, lanes), jnp.float32)
    gap = jnp.zeros((6, lanes), jnp.float32)
    potential = inner_order(potential_ref[...])
    for pair in range(dst_ref.shape[0] // 2):
        even = dst_ref[2 * pair]
        odd = dst_ref[2 * pair + 1]
        low, high = unfolded(even[50:76], odd[50:76])
        middle = jnp.concatenate([low[0:24], high], 0)
        for part, points in enumerate([even[0:50], middle, odd[0:50]]):
            tile = 3 * pair + part
            first, second, norm = split(jnp.concatenate([points, gap], 0))
            bias = potential[tile : tile + 1, :] * per_eps - 0.5 * norm
            extra = with_rows(first, 50, list(pieces(bias)) + [1.0, 1.0, 1.0])
            turned = jnp.concatenate([extra, pad, second, pad], 0).T
            column = lane_index(turned.shape)
            plain = jnp.where((column >= 50) & (column < 56), 0.0, turned)
            rows = slice(lanes * tile, lanes * (tile + 1))
            a_ref[rows, 0:lanes] = turned.astype(jnp.bfloat16)
            a_ref[rows, lanes : 2 * lanes] = plain.astype(jnp.bfloat16)


def dot(left, right):
    return jnp.dot(left, right, preferred_element_type=jnp.float32)


def biased_rows(rows16, bias):
    block = with_rows(rows16.astype(jnp.float32), 5, pieces(bias))
    return block.astype(jnp.bfloat16)


def as_tiles(row):
    return jnp.concatenate(
        [row[:, lanes * k : lanes * (k + 1)] for k in range(row.shape[1] // lanes)], 0
    )


def as_row(tiles):
    return jnp.concatenate([tiles[k : k + 1, :] for k in range(tiles.shape[0])], 1)


def source_kernel(src_ref, dst_ref, potential_ref, lse_ref, a_ref, b_ref, norm_ref, sum_ref):
    build_sources(src_ref, b_ref, norm_ref)
    build_targets(dst_ref, potential_ref, a_ref)
    targets = a_ref.shape[0]
    sources = b_ref.shape[1]
    width = 256
    shift = jnp.concatenate(
        [
            jnp.max(dot(a_ref[0:lanes, :], b_ref[:, width * n : width * (n + 1)]), 0, keepdims=True)
            for n in range(sources // width)
        ],
        1,
    )
    b_ref[48:64, :] = biased_rows(b_ref[48:64, :], -shift)
    for n in range(sources // width):
        columns = slice(width * n, width * (n + 1))
        terms = jnp.exp2(dot(a_ref[...], b_ref[:, columns]))
        total = jnp.sum(terms.reshape(targets // 8, 8, width), 0)
        sum_ref[0:1, columns] = jnp.sum(total, 0, keepdims=True)
    total = sum_ref[0:1, :]
    sum_ref[1:2, :] = shift + jnp.log2(total)

    @pl.when(jnp.logical_not(jnp.max(jnp.where(total <= too_large, 0.0, 1.0)) < 0.5))
    def exact():
        for n in range(sources // width):
            columns = slice(width * n, width * (n + 1))
            block = b_ref[:, columns]

            def rows_of(step):
                return pl.ds(pl.multiple_of(step * lanes, lanes), lanes)

            def highest(step, high):
                scores = dot(a_ref[rows_of(step), :], block)
                return jnp.maximum(high, jnp.max(scores, 0, keepdims=True))

            high = lax.fori_loop(
                0, targets // lanes, highest, jnp.full((1, width), -jnp.inf, jnp.float32)
            )

            def add(step, total):
                scores = dot(a_ref[rows_of(step), :], block)
                return total + jnp.sum(jnp.exp2(scores - high), 0, keepdims=True)

            total = lax.fori_loop(0, targets // lanes, add, jnp.zeros((1, width), jnp.float32))
            sum_ref[1:2, columns] = shift[:, columns] + (high + jnp.log2(total))

    lse_ref[...] = jnp.broadcast_to(as_tiles(sum_ref[1:2, :])[None], lse_ref.shape)


def target_kernel(lse_ref, log_a_ref, norm_ref, a_ref, b_ref, src_out, lse_out, acc_ref):
    targets = a_ref.shape[0]
    sources = b_ref.shape[1]
    width = 256
    parts = lse_ref[...]
    high = jnp.max(parts, 0)
    lse = high + jnp.log2(jnp.sum(jnp.exp2(parts - high[None]), 0))
    src_out[...] = epsilon * log_a_ref[...] - eps_ln2 * (lse - 0.5 * norm_ref[...])
    middle = biased_rows(b_ref[48:64, :], as_row(log2e * log_a_ref[...] - lse))

    def block_of(n):
        columns = slice(width * n, width * (n + 1))
        return jnp.concatenate(
            [b_ref[0:48, columns], middle[:, columns], b_ref[64:depth, columns]], 0
        )

    for n in range(sources // width):
        terms = jnp.exp2(dot(a_ref[...], block_of(n)))
        terms = terms[:, 0:lanes] + terms[:, lanes:]
        acc_ref[...] = terms if n == 0 else acc_ref[...] + terms
    totals = jnp.concatenate(
        [
            jnp.sum(acc_ref[lanes * t : lanes * (t + 1), :].T, 0, keepdims=True)
            for t in range(targets // lanes)
        ],
        0,
    )
    lse_out[...] = jnp.broadcast_to(jnp.log2(totals)[None], lse_out.shape)

    @pl.when(jnp.logical_not(jnp.max(jnp.where(totals >= too_small, 0.0, 1.0)) < 0.5))
    def exact():
        def one(tile, carry):
            left = a_ref[pl.ds(pl.multiple_of(tile * lanes, lanes), lanes), :]
            high = jnp.full((lanes, 1), -jnp.inf, jnp.float32)
            for n in range(sources // width):
                scores = dot(left, block_of(n))
                high = jnp.maximum(high, jnp.max(scores, 1, keepdims=True))
            total = jnp.zeros((lanes, 1), jnp.float32)
            for n in range(sources // width):
                scores = dot(left, block_of(n))
                total = total + jnp.sum(jnp.exp2(scores - high), 1, keepdims=True)
            result = jnp.broadcast_to(high + jnp.log2(total), (lanes, lanes)).T
            lse_out[:, pl.ds(tile, 1), :] = jnp.broadcast_to(
                result[None, 0:1, :], (lse_out.shape[0], 1, lanes)
            )
            return carry

        lax.fori_loop(0, targets // lanes, one, 0)


def join_kernel(lse_ref, log_b_ref, potential_ref, out_ref):
    parts = lse_ref[...]
    high = jnp.max(parts, 0)
    lse = high + jnp.log2(jnp.sum(jnp.exp2(parts - high[None]), 0))
    out_ref[...] = (
        epsilon * log_b_ref[...] + potential_ref[...] - eps_ln2 * outer_order(lse)
    )


def shape(*dims, dtype=jnp.float32):
    return jax.ShapeDtypeStruct(dims, dtype)


def call(kernel, outs, scratch=(), cost=None, ins=None, limit=vmem_limit):
    vmem = pl.BlockSpec(memory_space=pltpu.VMEM)
    many = isinstance(outs, tuple)
    return pl.pallas_call(
        kernel,
        out_shape=outs,
        out_specs=tuple(vmem for _ in outs) if many else vmem,
        scratch_shapes=scratch,
        compiler_params=pltpu.CompilerParams(vmem_limit_bytes=limit),
        cost_estimate=cost,
        **({} if ins is None else {"in_specs": ins}),
    )


def local(src_points, dst_points, log_a, log_b, dst_potential):
    rows = lax.axis_size("row")
    cols = lax.axis_size("col")
    sources = log_a.shape[0]
    targets = log_b.shape[0]
    log_a = log_a.reshape(sources // lanes, lanes)
    log_b = log_b.reshape(targets // lanes, lanes)
    potential = dst_potential.reshape(targets // lanes, lanes)
    pairs = sources * targets
    cost = pl.CostEstimate(
        flops=2 * depth * pairs, transcendentals=pairs, bytes_accessed=4 * depth * (sources + targets)
    )

    src, dst = call(
        pack_kernel,
        (shape(cols, 32, lanes), shape(80, lanes)),
        [
            pltpu.VMEM(src_points.shape, jnp.float32),
            pltpu.VMEM(dst_points.shape, jnp.float32),
            pltpu.SemaphoreType.DMA,
            pltpu.SemaphoreType.DMA,
        ],
        ins=[pl.BlockSpec(memory_space=pl.ANY)] * 2,
        limit=vmem_whole,
    )(src_points, dst_points)
    src = lax.all_to_all(src, "col", 0, 0, tiled=True)
    dst = lax.all_gather(dst, "row")

    lse, a, b, norms = call(
        source_kernel,
        (
            shape(cols, sources // lanes, lanes),
            shape(targets, depth, dtype=jnp.bfloat16),
            shape(depth, sources, dtype=jnp.bfloat16),
            shape(sources // lanes, lanes),
        ),
        [pltpu.VMEM((8, sources), jnp.float32)],
        cost,
    )(src, dst, potential)

    lse = lax.all_to_all(lse, "col", 0, 0, tiled=True)
    src_potential, lse = call(
        target_kernel,
        (shape(sources // lanes, lanes), shape(rows, targets // lanes, lanes)),
        [pltpu.VMEM((targets, lanes), jnp.float32)],
        cost,
    )(lse, log_a, norms, a, b)

    lse = lax.all_to_all(lse, "row", 0, 0, tiled=True)
    new_potential = call(join_kernel, shape(targets // lanes, lanes))(lse, log_b, potential)
    return src_potential.reshape(sources), new_potential.reshape(targets)


def solution(mesh):
    return jax.shard_map(
        local,
        mesh=mesh,
        in_specs=(P(None, ("row", "col")), P(None, ("col", "row")), P("row"), P("col"), P("col")),
        out_specs=(P("row"), P("col")),
        check_vma=False,
    )
```

```python
import math

import jax
import jax.numpy as jnp
from jax import lax
from jax.experimental import pallas as pl
from jax.experimental.pallas import tpu as pltpu
from jax.sharding import PartitionSpec as P

epsilon = 0.5
per_eps = math.log2(math.e) / epsilon
point_scale = math.sqrt(2.0 * per_eps)
eps_ln2 = epsilon * math.log(2.0)
log2e = math.log2(math.e)
too_large = 2.0**40
too_small = 2.0**-50
vmem_limit = 8 * 1024 * 1024
vmem_whole = 60 * 1024 * 1024

lanes = 128
half = 64
depth = 256
width = 256


def lane_index(shape):
    return lax.broadcasted_iota(jnp.int32, shape, 1)


def row_index(shape):
    return lax.broadcasted_iota(jnp.int32, shape, 0)


def rounded(value):
    return value.astype(jnp.bfloat16).astype(jnp.float32)


def pieces(value):
    first = rounded(value)
    second = rounded(value - first)
    third = rounded(value - first - second)
    return first, second, third


def folded(points, spare):
    left = jnp.concatenate([points[0:24], spare, jnp.zeros((1, half), jnp.float32)], 0)
    return jnp.concatenate([left, points[24:50]], 1)


def unfolded(first, second):
    left = lane_index(first.shape) < half
    low = jnp.where(left, first, swapped(second))
    high = jnp.where(left, swapped(first), second)
    return low, high


def pack_kernel(
    src_hbm,
    dst_hbm,
    log_a_hbm,
    potential_hbm,
    src_out,
    dst_out,
    src_ref,
    dst_ref,
    log_a_ref,
    potential_ref,
    sems,
):
    copies = [
        pltpu.make_async_copy(source, target, sems.at[k])
        for k, (source, target) in enumerate(
            [
                (src_hbm, src_ref),
                (dst_hbm, dst_ref),
                (log_a_hbm, log_a_ref),
                (potential_hbm, potential_ref),
            ]
        )
    ]
    for copy in copies:
        copy.start()
    for copy in copies:
        copy.wait()
    col = lax.axis_index("col")
    line = log_a_ref[pl.ds(lax.div(col, 2), 1), :]
    line = jnp.where(lax.rem(col, 2) == 1, swapped(line), line)
    src = folded(src_ref[...], line[:, :half])
    src = jnp.concatenate([src, jnp.zeros((6, lanes), jnp.float32)], 0)
    src_out[...] = jnp.broadcast_to(src[None], src_out.shape)
    row = lax.axis_index("row")
    odd = lax.rem(row, 2) == 1
    base = 3 * lax.div(row, 2)
    first, second, third = [potential_ref[pl.ds(base + k, 1), :] for k in range(3)]
    left = lane_index((1, lanes)) < half
    whole = jnp.where(odd, swapped(jnp.where(left, third, second)), first)
    rest = jnp.where(odd, swapped(third), second)
    dst_out[0:50, :] = dst_ref[:, :lanes]
    dst_out[50:76, :] = folded(dst_ref[:, lanes:], rest[:, :half])
    dst_out[76:80, :] = jnp.concatenate([whole, jnp.zeros((3, lanes), jnp.float32)], 0)


def swapped(rows):
    return pltpu.roll(rows, half, 1)


def outer_order(tiles):
    left = lane_index((1, lanes)) < half
    turned = swapped(tiles)
    rows = []
    for t in range(0, tiles.shape[0], 3):
        second, third = tiles[t + 1 : t + 2], turned[t + 2 : t + 3]
        rows.append(tiles[t : t + 1])
        rows.append(jnp.where(left, second, third))
        rows.append(jnp.where(left, third, second))
    return jnp.concatenate(rows, 0)


def split(points):
    scaled = points * point_scale
    high = rounded(scaled)
    low = rounded(scaled - high)
    exact = high + low
    return high, low, jnp.sum(exact * exact, 0, keepdims=True)


def with_rows(block, first, values):
    rows = row_index(block.shape)
    for offset, value in enumerate(values):
        block = jnp.where(rows == first + offset, value, block)
    return block


def build_sources(src_ref, b_ref, norm_ref, log_a_ref):
    pad = jnp.zeros((8, lanes), jnp.float32)
    norms, weights = [], []
    for k in range(src_ref.shape[0] // 2):
        low, high = unfolded(src_ref[2 * k], src_ref[2 * k + 1])
        first, second, norm = split(jnp.concatenate([low[0:24], high], 0))
        norms.append(norm)
        weights.append(low[24:25])
        extra = with_rows(first, 50, [1.0, 1.0, 1.0])
        columns = slice(lanes * k, lanes * (k + 1))
        second = jnp.concatenate([second, pad], 0).astype(jnp.bfloat16)
        b_ref[0:64, columns] = jnp.concatenate([extra, pad], 0).astype(jnp.bfloat16)
        b_ref[64:128, columns] = jnp.concatenate([first, pad], 0).astype(jnp.bfloat16)
        b_ref[128:192, columns] = second
        b_ref[192:256, columns] = second
    norm_ref[...] = jnp.concatenate(norms, 0)
    log_a_ref[...] = jnp.concatenate(weights, 0)


def build_targets(dst_ref, a_ref):
    pad = jnp.zeros((8, lanes), jnp.float32)
    gap = jnp.zeros((6, lanes), jnp.float32)
    for pair in range(dst_ref.shape[0] // 2):
        even = dst_ref[2 * pair]
        odd = dst_ref[2 * pair + 1]
        low, high = unfolded(even[50:76], odd[50:76])
        middle = jnp.concatenate([low[0:24], high], 0)
        groups = [(even[0:50], even[76:77]), (middle, low[24:25]), (odd[0:50], odd[76:77])]
        for part, (points, potential) in enumerate(groups):
            tile = 3 * pair + part
            first, second, norm = split(jnp.concatenate([points, gap], 0))
            bias = potential * per_eps - 0.5 * norm
            extra = with_rows(first, 50, pieces(bias))
            turned = jnp.concatenate([extra, pad, second, pad], 0).T
            column = lane_index(turned.shape)
            plain = jnp.where((column >= 50) & (column < 53), 0.0, turned)
            rows = slice(lanes * tile, lanes * (tile + 1))
            a_ref[rows, 0:lanes] = turned.astype(jnp.bfloat16)
            a_ref[rows, lanes : 2 * lanes] = plain.astype(jnp.bfloat16)


def dot(left, right):
    return jnp.dot(left, right, preferred_element_type=jnp.float32)


def as_tiles(row):
    return jnp.concatenate(
        [row[:, lanes * k : lanes * (k + 1)] for k in range(row.shape[1] // lanes)], 0
    )


def as_row(tiles):
    return jnp.concatenate([tiles[k : k + 1, :] for k in range(tiles.shape[0])], 1)


def unit_block(n):
    return slice(width * n, width * (n + 1))


def source_kernel(
    src_ref, dst_ref, lse_ref, share_ref, a_ref, b_ref, norm_ref, row_ref, log_a_ref
):
    build_sources(src_ref, b_ref, norm_ref, log_a_ref)
    build_targets(dst_ref, a_ref)
    targets = a_ref.shape[0]
    blocks = b_ref.shape[1] // width
    worst = jnp.zeros((1, width), jnp.float32)
    for n in range(blocks):
        scores = dot(a_ref[...], b_ref[:, unit_block(n)])
        shift = jnp.max(scores[0:lanes], 0, keepdims=True)
        terms = jnp.exp2(scores - shift)
        share_ref[:, unit_block(n)] = terms
        total = jnp.sum(jnp.sum(terms.reshape(targets // 8, 8, width), 0), 0, keepdims=True)
        worst = jnp.maximum(worst, jnp.where(total <= too_large, 0.0, 1.0))
        row_ref[0:1, unit_block(n)] = shift
        row_ref[1:2, unit_block(n)] = shift + jnp.log2(total)

    @pl.when(jnp.max(worst) > 0.5)
    def exact():
        def rows_of(step):
            return pl.ds(pl.multiple_of(step * lanes, lanes), lanes)

        for n in range(blocks):
            block = b_ref[:, unit_block(n)]

            def highest(step, high):
                scores = dot(a_ref[rows_of(step), :], block)
                return jnp.maximum(high, jnp.max(scores, 0, keepdims=True))

            high = lax.fori_loop(
                0, targets // lanes, highest, jnp.full((1, width), -jnp.inf, jnp.float32)
            )

            def add(step, total):
                terms = jnp.exp2(dot(a_ref[rows_of(step), :], block) - high)
                share_ref[rows_of(step), unit_block(n)] = terms
                return total + jnp.sum(terms, 0, keepdims=True)

            total = lax.fori_loop(0, targets // lanes, add, jnp.zeros((1, width), jnp.float32))
            row_ref[0:1, unit_block(n)] = high
            row_ref[1:2, unit_block(n)] = high + jnp.log2(total)

    lse_ref[...] = jnp.broadcast_to(as_tiles(row_ref[1:2, :])[None], lse_ref.shape)


def target_kernel(
    lse_ref, log_a_ref, norm_ref, row_ref, share_ref, a_ref, b_ref, src_out, lse_out
):
    targets, sources = share_ref.shape
    parts = lse_ref[...]
    high = jnp.max(parts, 0)
    lse = high + jnp.log2(jnp.sum(jnp.exp2(parts - high[None]), 0))
    src_out[...] = epsilon * log_a_ref[...] - eps_ln2 * (lse - 0.5 * norm_ref[...])
    bias = log2e * log_a_ref[...] - lse
    factor = jnp.exp2(bias + as_tiles(row_ref[0:1, :]))
    totals = []
    for t in range(targets // lanes):
        rows = slice(lanes * t, lanes * (t + 1))
        block = jnp.zeros((lanes, lanes), jnp.float32)
        for k in range(sources // lanes):
            block = block + share_ref[rows, lanes * k : lanes * (k + 1)] * factor[k : k + 1, :]
        totals.append(jnp.sum(block.T, 0, keepdims=True))
    totals = jnp.concatenate(totals, 0)
    lse_out[...] = jnp.broadcast_to(jnp.log2(totals)[None], lse_out.shape)

    @pl.when(jnp.max(jnp.where(totals >= too_small, 0.0, 1.0)) > 0.5)
    def exact():
        bias_row = as_row(bias)

        def one(tile, carry):
            left = a_ref[pl.ds(pl.multiple_of(tile * lanes, lanes), lanes), :]
            high = jnp.full((lanes, 1), -jnp.inf, jnp.float32)
            for n in range(sources // width):
                scores = dot(left, b_ref[:, unit_block(n)]) + bias_row[:, unit_block(n)]
                high = jnp.maximum(high, jnp.max(scores, 1, keepdims=True))
            total = jnp.zeros((lanes, 1), jnp.float32)
            for n in range(sources // width):
                scores = dot(left, b_ref[:, unit_block(n)]) + bias_row[:, unit_block(n)]
                total = total + jnp.sum(jnp.exp2(scores - high), 1, keepdims=True)
            result = jnp.broadcast_to(high + jnp.log2(total), (lanes, lanes)).T
            lse_out[:, pl.ds(tile, 1), :] = jnp.broadcast_to(
                result[None, 0:1, :], (lse_out.shape[0], 1, lanes)
            )
            return carry

        lax.fori_loop(0, targets // lanes, one, 0)


def join_kernel(lse_ref, log_b_ref, potential_ref, out_ref):
    parts = lse_ref[...]
    high = jnp.max(parts, 0)
    lse = high + jnp.log2(jnp.sum(jnp.exp2(parts - high[None]), 0))
    out_ref[...] = (
        epsilon * log_b_ref[...] + potential_ref[...] - eps_ln2 * outer_order(lse)
    )


def shape(*dims, dtype=jnp.float32):
    return jax.ShapeDtypeStruct(dims, dtype)


def call(kernel, outs, scratch=(), cost=None, limit=vmem_limit, **kwargs):
    vmem = pl.BlockSpec(memory_space=pltpu.VMEM)
    many = isinstance(outs, tuple)
    return pl.pallas_call(
        kernel,
        out_shape=outs,
        out_specs=tuple(vmem for _ in outs) if many else vmem,
        scratch_shapes=scratch,
        compiler_params=pltpu.CompilerParams(vmem_limit_bytes=limit),
        cost_estimate=cost,
        **kwargs,
    )


def local(src_points, dst_points, log_a, log_b, dst_potential):
    rows = lax.axis_size("row")
    cols = lax.axis_size("col")
    sources = log_a.shape[0]
    targets = log_b.shape[0]
    log_a = log_a.reshape(sources // lanes, lanes)
    log_b = log_b.reshape(targets // lanes, lanes)
    potential = dst_potential.reshape(targets // lanes, lanes)
    pairs = sources * targets
    cost = pl.CostEstimate(
        flops=2 * depth * pairs, transcendentals=pairs, bytes_accessed=4 * depth * (sources + targets)
    )

    packed = (src_points, dst_points, log_a, potential)
    src, dst = call(
        pack_kernel,
        (shape(cols, 32, lanes), shape(80, lanes)),
        [pltpu.VMEM(array.shape, jnp.float32) for array in packed]
        + [pltpu.SemaphoreType.DMA((len(packed),))],
        limit=vmem_whole,
        in_specs=[pl.BlockSpec(memory_space=pltpu.HBM)] * len(packed),
    )(*packed)
    src = lax.all_to_all(src, "col", 0, 0, tiled=True)
    dst = lax.all_gather(dst, "row")

    lse, share, a, b, norms, row, log_a = call(
        source_kernel,
        (
            shape(cols, sources // lanes, lanes),
            shape(targets, sources),
            shape(targets, depth, dtype=jnp.bfloat16),
            shape(depth, sources, dtype=jnp.bfloat16),
            shape(sources // lanes, lanes),
            shape(8, sources),
            shape(sources // lanes, lanes),
        ),
        (),
        cost,
    )(src, dst)

    lse = lax.all_to_all(lse, "col", 0, 0, tiled=True)
    src_potential, lse = call(
        target_kernel,
        (shape(sources // lanes, lanes), shape(rows, targets // lanes, lanes)),
        (),
        cost,
    )(lse, log_a, norms, row, share, a, b)

    lse = lax.all_to_all(lse, "row", 0, 0, tiled=True)
    new_potential = call(join_kernel, shape(targets // lanes, lanes))(lse, log_b, potential)
    return src_potential.reshape(sources), new_potential.reshape(targets)


def solution(mesh):
    return jax.shard_map(
        local,
        mesh=mesh,
        in_specs=(P(None, ("row", "col")), P(None, ("col", "row")), P("row"), P("col"), P("col")),
        out_specs=(P("row"), P("col")),
        check_vma=False,
    )
```

```python
import math

import jax
import jax.numpy as jnp
from jax import lax
from jax.experimental import pallas as pl
from jax.experimental.pallas import tpu as pltpu
from jax.sharding import PartitionSpec as P

epsilon = 0.5
per_eps = math.log2(math.e) / epsilon
point_scale = math.sqrt(2.0 * per_eps)
eps_ln2 = epsilon * math.log(2.0)
log2e = math.log2(math.e)
too_large = 2.0**40
too_small = 2.0**-50
vmem_limit = 8 * 1024 * 1024
vmem_whole = 60 * 1024 * 1024

lanes = 128
half = 64
depth = 256
width = 256


def lane_index(shape):
    return lax.broadcasted_iota(jnp.int32, shape, 1)


def row_index(shape):
    return lax.broadcasted_iota(jnp.int32, shape, 0)


def rounded(value):
    return value.astype(jnp.bfloat16).astype(jnp.float32)


def pieces(value):
    first = rounded(value)
    second = rounded(value - first)
    third = rounded(value - first - second)
    return first, second, third


def folded(points, spare):
    left = jnp.concatenate([points[0:24], spare, jnp.zeros((1, half), jnp.float32)], 0)
    return jnp.concatenate([left, points[24:50]], 1)


def unfolded(first, second):
    left = lane_index(first.shape) < half
    low = jnp.where(left, first, swapped(second))
    high = jnp.where(left, swapped(first), second)
    return low, high


def pack_kernel(
    src_hbm,
    dst_hbm,
    log_a_hbm,
    potential_hbm,
    src_out,
    dst_out,
    src_ref,
    dst_ref,
    log_a_ref,
    potential_ref,
    sems,
):
    copies = [
        pltpu.make_async_copy(source, target, sems.at[k])
        for k, (source, target) in enumerate(
            [
                (src_hbm, src_ref),
                (dst_hbm, dst_ref),
                (log_a_hbm, log_a_ref),
                (potential_hbm, potential_ref),
            ]
        )
    ]
    for copy in copies:
        copy.start()
    for copy in copies:
        copy.wait()
    col = lax.axis_index("col")
    line = log_a_ref[pl.ds(lax.div(col, 2), 1), :]
    line = jnp.where(lax.rem(col, 2) == 1, swapped(line), line)
    src = folded(src_ref[...], line[:, :half])
    src = jnp.concatenate([src, jnp.zeros((6, lanes), jnp.float32)], 0)
    src_out[...] = jnp.broadcast_to(src[None], src_out.shape)
    row = lax.axis_index("row")
    odd = lax.rem(row, 2) == 1
    base = 3 * lax.div(row, 2)
    first, second, third = [potential_ref[pl.ds(base + k, 1), :] for k in range(3)]
    left = lane_index((1, lanes)) < half
    whole = jnp.where(odd, swapped(jnp.where(left, third, second)), first)
    rest = jnp.where(odd, swapped(third), second)
    dst_out[0:50, :] = dst_ref[:, :lanes]
    dst_out[50:76, :] = folded(dst_ref[:, lanes:], rest[:, :half])
    dst_out[76:80, :] = jnp.concatenate([whole, jnp.zeros((3, lanes), jnp.float32)], 0)


def swapped(rows):
    return pltpu.roll(rows, half, 1)


def outer_order(tiles):
    left = lane_index((1, lanes)) < half
    turned = swapped(tiles)
    rows = []
    for t in range(0, tiles.shape[0], 3):
        second, third = tiles[t + 1 : t + 2], turned[t + 2 : t + 3]
        rows.append(tiles[t : t + 1])
        rows.append(jnp.where(left, second, third))
        rows.append(jnp.where(left, third, second))
    return jnp.concatenate(rows, 0)


def split(points):
    scaled = points * point_scale
    high = rounded(scaled)
    low = rounded(scaled - high)
    exact = high + low
    return high, low, jnp.sum(exact * exact, 0, keepdims=True)


def with_rows(block, first, values):
    rows = row_index(block.shape)
    for offset, value in enumerate(values):
        block = jnp.where(rows == first + offset, value, block)
    return block


def build_sources(src_ref, b_ref, norm_ref, log_a_ref):
    pad = jnp.zeros((8, lanes), jnp.float32)
    norms, weights = [], []
    for k in range(src_ref.shape[0] // 2):
        low, high = unfolded(src_ref[2 * k], src_ref[2 * k + 1])
        first, second, norm = split(jnp.concatenate([low[0:24], high], 0))
        norms.append(norm)
        weights.append(low[24:25])
        extra = with_rows(first, 50, [1.0, 1.0, 1.0])
        columns = slice(lanes * k, lanes * (k + 1))
        second = jnp.concatenate([second, pad], 0).astype(jnp.bfloat16)
        b_ref[0:64, columns] = jnp.concatenate([extra, pad], 0).astype(jnp.bfloat16)
        b_ref[64:128, columns] = jnp.concatenate([first, pad], 0).astype(jnp.bfloat16)
        b_ref[128:192, columns] = second
        b_ref[192:256, columns] = second
    norm_ref[...] = jnp.concatenate(norms, 0)
    log_a_ref[...] = jnp.concatenate(weights, 0)


def build_targets(dst_ref, a_ref):
    pad = jnp.zeros((8, lanes), jnp.float32)
    gap = jnp.zeros((6, lanes), jnp.float32)
    for pair in range(dst_ref.shape[0] // 2):
        even = dst_ref[2 * pair]
        odd = dst_ref[2 * pair + 1]
        low, high = unfolded(even[50:76], odd[50:76])
        middle = jnp.concatenate([low[0:24], high], 0)
        groups = [(even[0:50], even[76:77]), (middle, low[24:25]), (odd[0:50], odd[76:77])]
        for part, (points, potential) in enumerate(groups):
            tile = 3 * pair + part
            first, second, norm = split(jnp.concatenate([points, gap], 0))
            bias = potential * per_eps - 0.5 * norm
            extra = with_rows(first, 50, pieces(bias))
            turned = jnp.concatenate([extra, pad, second, pad], 0).T
            column = lane_index(turned.shape)
            plain = jnp.where((column >= 50) & (column < 53), 0.0, turned)
            rows = slice(lanes * tile, lanes * (tile + 1))
            a_ref[rows, 0:lanes] = turned.astype(jnp.bfloat16)
            a_ref[rows, lanes : 2 * lanes] = plain.astype(jnp.bfloat16)


def dot(left, right):
    return jnp.dot(left, right, preferred_element_type=jnp.float32)


def as_tiles(row):
    return jnp.concatenate(
        [row[:, lanes * k : lanes * (k + 1)] for k in range(row.shape[1] // lanes)], 0
    )


def as_row(tiles):
    return jnp.concatenate([tiles[k : k + 1, :] for k in range(tiles.shape[0])], 1)


def unit_block(n):
    return slice(width * n, width * (n + 1))


def source_kernel(
    src_ref, dst_ref, lse_ref, share_ref, a_ref, b_ref, norm_ref, row_ref, log_a_ref
):
    build_sources(src_ref, b_ref, norm_ref, log_a_ref)
    build_targets(dst_ref, a_ref)
    targets = a_ref.shape[0]
    blocks = b_ref.shape[1] // width
    worst = jnp.zeros((1, width), jnp.float32)
    for n in range(blocks):
        scores = dot(a_ref[...], b_ref[:, unit_block(n)])
        shift = jnp.max(scores[0:lanes], 0, keepdims=True)
        terms = jnp.exp2(scores - shift)
        share_ref[:, unit_block(n)] = terms
        total = jnp.sum(jnp.sum(terms.reshape(targets // 8, 8, width), 0), 0, keepdims=True)
        worst = jnp.maximum(worst, jnp.where(total <= too_large, 0.0, 1.0))
        row_ref[0:1, unit_block(n)] = shift
        row_ref[1:2, unit_block(n)] = shift + jnp.log2(total)

    @pl.when(jnp.max(worst) > 0.5)
    def exact():
        def rows_of(step):
            return pl.ds(pl.multiple_of(step * lanes, lanes), lanes)

        for n in range(blocks):
            block = b_ref[:, unit_block(n)]

            def highest(step, high):
                scores = dot(a_ref[rows_of(step), :], block)
                return jnp.maximum(high, jnp.max(scores, 0, keepdims=True))

            high = lax.fori_loop(
                0, targets // lanes, highest, jnp.full((1, width), -jnp.inf, jnp.float32)
            )

            def add(step, total):
                terms = jnp.exp2(dot(a_ref[rows_of(step), :], block) - high)
                share_ref[rows_of(step), unit_block(n)] = terms
                return total + jnp.sum(terms, 0, keepdims=True)

            total = lax.fori_loop(0, targets // lanes, add, jnp.zeros((1, width), jnp.float32))
            row_ref[0:1, unit_block(n)] = high
            row_ref[1:2, unit_block(n)] = high + jnp.log2(total)

    lse_ref[...] = jnp.broadcast_to(as_tiles(row_ref[1:2, :])[None], lse_ref.shape)


def target_kernel(
    lse_ref, log_a_ref, norm_ref, row_ref, share_ref, a_ref, b_ref, src_out, lse_out
):
    targets, sources = share_ref.shape
    parts = lse_ref[...]
    high = jnp.max(parts, 0)
    lse = high + jnp.log2(jnp.sum(jnp.exp2(parts - high[None]), 0))
    src_out[...] = epsilon * log_a_ref[...] - eps_ln2 * (lse - 0.5 * norm_ref[...])
    bias = log2e * log_a_ref[...] - lse
    factor = jnp.exp2(bias + as_tiles(row_ref[0:1, :]))
    totals = []
    for t in range(targets // lanes):
        rows = slice(lanes * t, lanes * (t + 1))
        block = jnp.zeros((lanes, lanes), jnp.float32)
        for k in range(sources // lanes):
            block = block + share_ref[rows, lanes * k : lanes * (k + 1)] * factor[k : k + 1, :]
        totals.append(jnp.sum(block.T, 0, keepdims=True))
    totals = jnp.concatenate(totals, 0)
    lse_out[...] = jnp.broadcast_to(jnp.log2(totals)[None], lse_out.shape)

    @pl.when(jnp.max(jnp.where(totals >= too_small, 0.0, 1.0)) > 0.5)
    def exact():
        bias_row = as_row(bias)

        def one(tile, carry):
            left = a_ref[pl.ds(pl.multiple_of(tile * lanes, lanes), lanes), :]
            high = jnp.full((lanes, 1), -jnp.inf, jnp.float32)
            for n in range(sources // width):
                scores = dot(left, b_ref[:, unit_block(n)]) + bias_row[:, unit_block(n)]
                high = jnp.maximum(high, jnp.max(scores, 1, keepdims=True))
            total = jnp.zeros((lanes, 1), jnp.float32)
            for n in range(sources // width):
                scores = dot(left, b_ref[:, unit_block(n)]) + bias_row[:, unit_block(n)]
                total = total + jnp.sum(jnp.exp2(scores - high), 1, keepdims=True)
            result = jnp.broadcast_to(high + jnp.log2(total), (lanes, lanes)).T
            lse_out[:, pl.ds(tile, 1), :] = jnp.broadcast_to(
                result[None, 0:1, :], (lse_out.shape[0], 1, lanes)
            )
            return carry

        lax.fori_loop(0, targets // lanes, one, 0)


def join_kernel(lse_ref, log_b_ref, potential_ref, out_ref):
    parts = lse_ref[...]
    high = jnp.max(parts, 0)
    lse = high + jnp.log2(jnp.sum(jnp.exp2(parts - high[None]), 0))
    out_ref[...] = (
        epsilon * log_b_ref[...] + potential_ref[...] - eps_ln2 * outer_order(lse)
    )


def listed_from(first, size):
    return [[(first + k) % size for k in range(size)]]


def shape(*dims, dtype=jnp.float32):
    return jax.ShapeDtypeStruct(dims, dtype)


def call(kernel, outs, scratch=(), cost=None, limit=vmem_limit, **kwargs):
    vmem = pl.BlockSpec(memory_space=pltpu.VMEM)
    many = isinstance(outs, tuple)
    return pl.pallas_call(
        kernel,
        out_shape=outs,
        out_specs=tuple(vmem for _ in outs) if many else vmem,
        scratch_shapes=scratch,
        compiler_params=pltpu.CompilerParams(vmem_limit_bytes=limit),
        cost_estimate=cost,
        **kwargs,
    )


def local(src_points, dst_points, log_a, log_b, dst_potential):
    rows = lax.axis_size("row")
    cols = lax.axis_size("col")
    sources = log_a.shape[0]
    targets = log_b.shape[0]
    log_a = log_a.reshape(sources // lanes, lanes)
    log_b = log_b.reshape(targets // lanes, lanes)
    potential = dst_potential.reshape(targets // lanes, lanes)
    pairs = sources * targets
    cost = pl.CostEstimate(
        flops=2 * depth * pairs, transcendentals=pairs, bytes_accessed=4 * depth * (sources + targets)
    )

    packed = (src_points, dst_points, log_a, potential)
    src, dst = call(
        pack_kernel,
        (shape(cols, 32, lanes), shape(80, lanes)),
        [pltpu.VMEM(array.shape, jnp.float32) for array in packed]
        + [pltpu.SemaphoreType.DMA((len(packed),))],
        limit=vmem_whole,
        in_specs=[pl.BlockSpec(memory_space=pltpu.HBM)] * len(packed),
    )(*packed)
    src = lax.all_to_all(src, "col", 0, 0, tiled=True)
    dst = lax.all_gather(dst, "row")

    lse, share, a, b, norms, row, log_a = call(
        source_kernel,
        (
            shape(cols, sources // lanes, lanes),
            shape(targets, sources),
            shape(targets, depth, dtype=jnp.bfloat16),
            shape(depth, sources, dtype=jnp.bfloat16),
            shape(sources // lanes, lanes),
            shape(8, sources),
            shape(sources // lanes, lanes),
        ),
        (),
        cost,
    )(src, dst)

    far = listed_from(cols // 2 + 2, cols)
    lse = lax.all_to_all(lse, "col", 0, 0, axis_index_groups=far, tiled=True)
    src_potential, lse = call(
        target_kernel,
        (shape(sources // lanes, lanes), shape(rows, targets // lanes, lanes)),
        (),
        cost,
    )(lse, log_a, norms, row, share, a, b)

    quarter = listed_from(rows // 4, rows)
    lse = lax.all_to_all(lse, "row", 0, 0, axis_index_groups=quarter, tiled=True)
    new_potential = call(join_kernel, shape(targets // lanes, lanes))(lse, log_b, potential)
    return src_potential.reshape(sources), new_potential.reshape(targets)


def solution(mesh):
    return jax.shard_map(
        local,
        mesh=mesh,
        in_specs=(P(None, ("row", "col")), P(None, ("col", "row")), P("row"), P("col"), P("col")),
        out_specs=(P("row"), P("col")),
        check_vma=False,
    )
```
